256 devices in a mesh: dp: 32 (over y, z), mp: 8 (over x, core).
Axes of the slice: x: 4, y: 4, z: 8, core: 2. Of those that a mesh axis runs over, the one named last changes fastest.
Arguments:
- activations: bfloat16 [46080, 8192], P('dp', 'mp'), may hold values from -6 to 6
- out_grads: bfloat16 [46080, 2048], P('dp'), may hold values from -0.15625 to 0.15625
- feedback: bfloat16 [32, 8192, 2048], P('dp', 'mp'), may hold values from -6 to 6
- q_prev: float32 [1024, 2, 32], replicated, may hold values from -0.1875 to 0.1875
Outputs:
- error_new: bfloat16 [32, 8192, 2048], P('dp', 'mp')
- q_new: float32 [1024, 2, 32], replicated
The draws below stay inside these ranges and needn't reach their ends.
All inputs are finite; a program needn't handle non-finite values.
Results may differ from the reference program's by a relative error of at most 0.001.
Values sent between devices are 32-bit elements; how exact they have to be, the bound alone decides.
A program may use at most 128 MiB of HBM per device.

```python
import jax
import jax.numpy as jnp
from jax import lax

D = 8192
KVW = 1024
R = 32
TOK_DEV = 1440
TOKENS = 46080
N_DP = 32


def levels(key, dims, split, smallest, top_value):
    def one(axis_at, shards_of):
        steps = jax.random.uniform(jax.random.fold_in(jax.random.fold_in(key, 6), axis_at), (shards_of,), jnp.float32, smallest / len(split), top_value / len(split))
        return jnp.repeat(jnp.exp(steps), dims[axis_at] // shards_of).reshape((-1,) + (1,) * (len(dims) - axis_at - 1))

    level = one(*split[0])
    for cut in split[1:]:
        level = level * one(*cut)
    return level


def scatter_about(own_key, shape, width, reach, cuts=(), held_as=jnp.bfloat16):
    array = width * jax.random.normal(own_key, shape, jnp.float32)
    if cuts:
        array = array * levels(own_key, shape, cuts, -0.22, 0.18)
    return jnp.clip(array, -reach, reach).astype(held_as)


def setup_inputs(seed: int = 0) -> dict:
    splits = jax.random.split(jax.random.key(seed), 5)
    activations = scatter_about(splits[0], (TOKENS, D), 1.0, 6.0, ((0, 32), (1, 8)))
    out_grads = scatter_about(splits[1], (TOKENS, 2 * KVW), TOK_DEV ** -0.5, 0.15625, ((0, 32),))
    feedback = scatter_about(splits[2], (N_DP, D, 2 * KVW), 1.0, 6.0, ((0, 32), (1, 8)))
    q_prev = scatter_about(splits[3], (KVW, 2, R), KVW ** -0.5, 0.1875, (), jnp.float32)
    return dict(activations=activations, out_grads=out_grads, feedback=feedback, q_prev=q_prev)


def gram_of(factor_rows):
    return jnp.einsum('dmr,dms->mrs', factor_rows, factor_rows, precision=lax.Precision.HIGHEST)

def orthonormal(factor_rows, factor_low):
    columns = []
    for which in range(factor_rows.shape[1]):
        solved = lax.linalg.triangular_solve(factor_low[which], factor_rows[:, which, :], left_side=False, lower=True, transpose_a=True)
        columns.append(solved)
    return jnp.stack(columns, axis=1)

def reference(activations, out_grads, feedback, q_prev):
    highest = lax.Precision.HIGHEST
    tok_blocks = activations.reshape(N_DP, TOK_DEV, D)
    grad_blocks = out_grads.reshape(N_DP, TOK_DEV, 2, KVW)

    def add_left(running, blocks):
        inputs, upstream, stored = blocks
        wide_inputs = inputs.astype(jnp.float32)
        grad_q = jnp.einsum('tmw,wmr->tmr', upstream.astype(jnp.float32), q_prev, precision=highest)
        summand = jnp.einsum('td,tmr->dmr', wide_inputs, grad_q, precision=highest)
        stored_three = stored.astype(jnp.float32).reshape(D, 2, KVW)
        summand = summand + jnp.einsum('dmw,wmr->dmr', stored_three, q_prev, precision=highest)
        return (running + summand, None)
    start_left = jnp.zeros((D, 2, R), jnp.float32)
    p_total, _ = lax.scan(add_left, start_left, (tok_blocks, grad_blocks, feedback))
    p_avg = p_total / N_DP
    factor_low = jnp.linalg.cholesky(gram_of(p_avg))
    p_hat = orthonormal(p_avg, factor_low)

    def add_right(running, blocks):
        inputs, upstream, stored = blocks
        projected = jnp.einsum('td,dmr->tmr', inputs.astype(jnp.float32), p_hat, precision=highest)
        summand = jnp.einsum('tmw,tmr->wmr', upstream.astype(jnp.float32), projected, precision=highest)
        stored_three = stored.astype(jnp.float32).reshape(D, 2, KVW)
        summand = summand + jnp.einsum('dmw,dmr->wmr', stored_three, p_hat, precision=highest)
        return (running + summand, None)
    start_right = jnp.zeros((KVW, 2, R), jnp.float32)
    q_total, _ = lax.scan(add_right, start_right, (tok_blocks, grad_blocks, feedback))
    q_new = q_total / N_DP
    rebuilt = jnp.einsum('dmr,wmr->dmw', p_hat, q_new, precision=highest).reshape(D, 2 * KVW)

    def replica_error(blocks):
        inputs, upstream, stored = blocks
        weight_grad = jnp.dot(inputs.T.astype(jnp.float32), upstream.reshape(TOK_DEV, 2 * KVW).astype(jnp.float32), preferred_element_type=jnp.float32)
        matrix = weight_grad + stored.astype(jnp.float32)
        return (matrix - rebuilt).astype(jnp.bfloat16)
    error_new = lax.map(replica_error, (tok_blocks, grad_blocks, feedback))
    return (error_new, q_new)
```

```python
import functools

import jax
import jax.numpy as jnp
from jax import lax
from jax.experimental import pallas as pl
from jax.experimental.pallas import tpu as pltpu
from jax.sharding import PartitionSpec as P

MESH = pl.DeviceIdType.MESH
F32 = jnp.float32
BF16 = jnp.bfloat16
HIGHEST = lax.Precision.HIGHEST

NY, NZ, NX, NC = 4, 8, 4, 2
TOK, ROWS, KVW, R = 1440, 1024, 1024, 32
TOK_PAD = 1536
WIDTH = 2 * KVW
CB = 8
CL = 256
N_PEERS = 31


def ring(step, size):
    return min(step, size - step)


DP_PEERS = sorted(
    [(a, b) for a in range(NY) for b in range(NZ) if (a, b) != (0, 0)],
    key=lambda o: -(ring(o[0], NY) + ring(o[1], NZ)),
)
BLOCK_PEERS = sorted(
    [(a, b, c) for a in range(NY) for b in range(NX) for c in range(NC) if (a, b, c) != (0, 0, 0)],
    key=lambda o: -(ring(o[0], NY) + ring(o[1], NX)),
)
Z_PEERS = sorted(range(1, NZ), key=lambda o: -ring(o, NZ))
MP_PEERS = sorted(
    [(b, c) for b in range(NX) for c in range(NC) if (b, c) != (0, 0)],
    key=lambda o: -ring(o[0], NX),
)


def split3(x):
    hi = x.astype(BF16)
    rest = x - hi.astype(F32)
    mid = rest.astype(BF16)
    low = (rest - mid.astype(F32)).astype(BF16)
    return hi, mid, low


def stack3(x):
    return jnp.concatenate(split3(x), axis=0)


def sum3(x):
    n = x.shape[0] // 3
    return x[:n] + (x[n : 2 * n] + x[2 * n :])


def dot(a, b, ca, cb):
    return lax.dot_general(a, b, (((ca,), (cb,)), ((), ())), preferred_element_type=F32)


def dot_high(a, b, ca, cb):
    return lax.dot_general(
        a, b, (((ca,), (cb,)), ((), ())), precision=HIGHEST, preferred_element_type=F32
    )


def chunk(index):
    row = pl.multiple_of((index // 4) * CB, CB)
    lane = pl.multiple_of(lax.rem(index, 4) * CL, CL)
    return pl.ds(row, CB), pl.ds(lane, CL)


def inverse_factors(gram):
    lane = lax.broadcasted_iota(jnp.int32, (R, 128), 1)
    row = lax.broadcasted_iota(jnp.int32, (R, 128), 0)
    first = lax.rem(lane // R, 2) == 0
    unit = jnp.where(lax.rem(lane, R) == row, 1.0, 0.0).astype(F32)
    w = jnp.where(lane < 2 * R, gram, unit)
    for k in range(R - 1):
        pivot_row = w[k : k + 1, :]
        f0 = w[:, k : k + 1] / pivot_row[:, k : k + 1]
        f1 = w[:, R + k : R + k + 1] / pivot_row[:, R + k : R + k + 1]
        factor = jnp.where(first, f0, f1)
        w = w - jnp.where(row > k, factor * pivot_row, 0.0)
    on0 = jnp.sum(jnp.where(lane == row, w, 0.0), axis=1, keepdims=True)
    on1 = jnp.sum(jnp.where(lane == row + R, w, 0.0), axis=1, keepdims=True)
    w = w * jnp.where(first, 1.0 / jnp.sqrt(on0), 1.0 / jnp.sqrt(on1))
    return w[:, 2 * R : 3 * R], w[:, 3 * R : 4 * R]


def kernel(
    a_hbm, g_hbm, f_hbm, qt_hbm, err_hbm, qn_ref,
    a, g, f, qt, at, mat, mhi, mlo, err, p_part, p_recv, p_full,
    gram_own, gram_recv, q_part, q_recv, z_sum, z_recv, q_full, phat,
    load_sem, out_sem, send_sem, recv_sem,
):
    dp, mp = lax.axis_index("dp"), lax.axis_index("mp")
    y, z, x, c = dp // NZ, lax.rem(dp, NZ), mp // NC, lax.rem(mp, NC)
    block_id = y * 8 + mp

    def dp_target(o):
        return (lax.rem(y + o[0], NY) * NZ + lax.rem(z + o[1], NZ), mp)

    def block_target(o):
        return (
            lax.rem(y + o[0], NY) * NZ + z,
            lax.rem(x + o[1], NX) * NC + lax.rem(c + o[2], NC),
        )

    def z_target(o):
        return (y * NZ + lax.rem(z + o, NZ), mp)

    barrier = pltpu.get_barrier_semaphore()
    greeted = [dp_target(o) for o in DP_PEERS]
    greeted += [block_target(o) for o in BLOCK_PEERS if o[1:] != (0, 0)]
    for target in greeted:
        pl.semaphore_signal(barrier, inc=1, device_id=target, device_id_type=MESH)

    loads = []

    def load(src, dst):
        copy = pltpu.make_async_copy(src, dst, load_sem.at[len(loads)])
        copy.start()
        loads.append(copy)
        return copy

    load_q = load(qt_hbm, qt)
    load_g = [
        load(g_hbm.at[:, pl.ds(m * KVW, KVW)], g.at[pl.ds(0, TOK), pl.ds(m * KVW, KVW)])
        for m in range(2)
    ]
    load_f = [load(f_hbm.at[:, pl.ds(m * KVW, KVW)], f.at[:, pl.ds(m * KVW, KVW)]) for m in range(2)]
    load_a = load(a_hbm, a.at[pl.ds(0, TOK), :])
    g[TOK:, :] = jnp.zeros((TOK_PAD - TOK, WIDTH), BF16)
    a[TOK:, :] = jnp.zeros((TOK_PAD - TOK, ROWS), BF16)

    load_q.wait()
    q3 = [stack3(qt[pl.ds(m * R, R), :]) for m in range(2)]
    inner = []
    for m in range(2):
        load_g[m].wait()
        inner.append(sum3(dot(q3[m], g[:, m * KVW : (m + 1) * KVW], 1, 1)))
    stored = []
    for m in range(2):
        load_f[m].wait()
        stored.append(sum3(dot(q3[m], f[:, m * KVW : (m + 1) * KVW], 1, 1)))
    load_a.wait()
    inner3 = stack3(jnp.concatenate(inner, axis=0))
    p_part[...] = sum3(dot(inner3, a[...], 1, 0)) + jnp.concatenate(stored, axis=0)

    pl.semaphore_wait(barrier, len(greeted))

    def send(src, dst, target, which):
        pltpu.make_async_remote_copy(
            src_ref=src,
            dst_ref=dst,
            send_sem=send_sem.at[which],
            recv_sem=recv_sem.at[which],
            device_id=target,
            device_id_type=MESH,
        ).start()

    def wait_on(sem, view):
        pltpu.make_async_copy(view, view, sem).wait()

    for i, o in enumerate(DP_PEERS):
        target = dp_target(o)
        row, lane = chunk(target[0])
        send(p_part.at[row, lane], p_recv.at[i], target, 0)

    at[...] = a[...].T

    def columns(n):
        lanes = pl.ds(pl.multiple_of(n * 256, 256), 256)
        block = dot(at[...], g[:, lanes], 1, 0) + f[:, lanes].astype(F32)
        mat[:, lanes] = block
        hi = block.astype(BF16)
        mhi[:, lanes] = hi
        mlo[:, lanes] = (block - hi.astype(F32)).astype(BF16)

    pl.loop(0, 4)(columns)

    wait_on(recv_sem.at[0], p_recv)
    row, lane = chunk(dp)
    p_own = p_part[row, lane]
    for i in range(N_PEERS):
        p_own = p_own + p_recv[i]
    p_full[row, lane] = p_own * (1.0 / 32)
    for o in DP_PEERS:
        send(p_full.at[row, lane], p_full.at[row, lane], dp_target(o), 1)

    pl.loop(4, 8)(columns)

    wait_on(recv_sem.at[1], p_recv)
    p_all = p_full[...]

    both = dot_high(p_all, p_all, 1, 1)
    lane64 = lax.broadcasted_iota(jnp.int32, (R, 2 * R), 1)
    terms = jnp.where(lane64 < R, both[:R], both[R:])
    gram_own[...] = jnp.concatenate([terms, jnp.zeros((R, 128 - 2 * R), F32)], axis=1)
    for o in MP_PEERS:
        send(gram_own, gram_recv.at[mp], block_target((0,) + o), 2)
    gram_recv[mp] = gram_own[...]

    for m in range(2):
        cols = slice(m * KVW, (m + 1) * KVW)
        p3 = stack3(p_all[m * R : (m + 1) * R])
        q_part[pl.ds(m * R, R), :] = sum3(dot(p3, mhi[:, cols], 1, 0) + dot(p3, mlo[:, cols], 1, 0))
    for i, o in enumerate(BLOCK_PEERS):
        target = block_target(o)
        row, lane = chunk((target[0] // NZ) * 8 + target[1])
        send(q_part.at[row, lane], q_recv.at[i], target, 3)

    wait_on(recv_sem.at[2], gram_recv.at[pl.ds(0, 7)])
    gram = gram_recv[0]
    for i in range(1, 8):
        gram = gram + gram_recv[i]
    inverses = inverse_factors(gram)

    wait_on(recv_sem.at[3], q_recv)
    row, lane = chunk(block_id)
    q_own = q_part[row, lane]
    for i in range(N_PEERS):
        q_own = q_own + q_recv[i]
    z_sum[...] = q_own
    for o in Z_PEERS:
        send(z_sum, z_recv.at[z], z_target(o), 4)
    z_recv[z] = q_own

    for m in range(2):
        normed = dot_high(inverses[m], p_all[m * R : (m + 1) * R], 1, 0)
        hi, low, _ = split3(normed)
        laid = jnp.concatenate([hi, low, hi, jnp.zeros_like(hi)], axis=0)
        phat[m] = laid.T

    wait_on(recv_sem.at[4], z_recv.at[pl.ds(0, 7)])
    q_own = z_recv[0]
    for i in range(1, NZ):
        q_own = q_own + z_recv[i]
    q_full[row, lane] = q_own * (1.0 / 32)
    for o in BLOCK_PEERS:
        send(q_full.at[row, lane], q_full.at[row, lane], block_target(o), 5)
    wait_on(recv_sem.at[5], q_recv)

    outs = []
    q_new = [dot_high(inverses[m], q_full[m * R : (m + 1) * R, :], 1, 0) for m in range(2)]
    laid = []
    for m in range(2):
        qn_ref[pl.ds(m * R, R), :] = q_new[m]
        hi, low, _ = split3(q_new[m])
        laid.append(jnp.concatenate([hi, hi, low, jnp.zeros_like(hi)], axis=0))
    for i in range(8):
        rows = pl.ds(i * 128, 128)
        for m in range(2):
            cols = slice(m * KVW, (m + 1) * KVW)
            rebuilt = dot(phat[m, rows, :], laid[m], 1, 0)
            err[rows, cols] = (mat[rows, cols] - rebuilt).astype(BF16)
        copy = pltpu.make_async_copy(err.at[rows, :], err_hbm.at[rows, :], out_sem.at[i])
        copy.start()
        outs.append(copy)

    wait_on(send_sem.at[0], p_recv)
    wait_on(send_sem.at[1], p_recv)
    wait_on(send_sem.at[2], gram_recv.at[pl.ds(0, 7)])
    wait_on(send_sem.at[3], q_recv)
    wait_on(send_sem.at[4], z_recv.at[pl.ds(0, 7)])
    wait_on(send_sem.at[5], q_recv)
    for copy in outs:
        copy.wait()


def per_device(activations, out_grads, feedback, q_prev):
    qt = jnp.transpose(q_prev, (1, 2, 0)).reshape(2 * R, KVW)
    any_space = pl.BlockSpec(memory_space=pl.ANY)
    err, qn = pl.pallas_call(
        kernel,
        out_shape=(
            jax.ShapeDtypeStruct((ROWS, WIDTH), BF16),
            jax.ShapeDtypeStruct((2 * R, KVW), F32),
        ),
        in_specs=[any_space] * 4,
        out_specs=(any_space, pl.BlockSpec(memory_space=pltpu.VMEM)),
        scratch_shapes=[
            pltpu.VMEM((TOK_PAD, ROWS), BF16),
            pltpu.VMEM((TOK_PAD, WIDTH), BF16),
            pltpu.VMEM((ROWS, WIDTH), BF16),
            pltpu.VMEM((2 * R, KVW), F32),
            pltpu.VMEM((ROWS, TOK_PAD), BF16),
            pltpu.VMEM((ROWS, WIDTH), F32),
            pltpu.VMEM((ROWS, WIDTH), BF16),
            pltpu.VMEM((ROWS, WIDTH), BF16),
            pltpu.VMEM((ROWS, WIDTH), BF16),
            pltpu.VMEM((2 * R, ROWS), F32),
            pltpu.VMEM((N_PEERS, CB, CL), F32),
            pltpu.VMEM((2 * R, ROWS), F32),
            pltpu.VMEM((R, 128), F32),
            pltpu.VMEM((8, R, 128), F32),
            pltpu.VMEM((2 * R, KVW), F32),
            pltpu.VMEM((N_PEERS, CB, CL), F32),
            pltpu.VMEM((CB, CL), F32),
            pltpu.VMEM((NZ, CB, CL), F32),
            pltpu.VMEM((2 * R, KVW), F32),
            pltpu.VMEM((2, ROWS, 128), BF16),
            pltpu.SemaphoreType.DMA((6,)),
            pltpu.SemaphoreType.DMA((8,)),
            pltpu.SemaphoreType.DMA((6,)),
            pltpu.SemaphoreType.DMA((6,)),
        ],
        compiler_params=pltpu.CompilerParams(
            collective_id=0, has_side_effects=True, vmem_limit_bytes=60 * 2**20
        ),
    )(activations, out_grads, feedback[0], qt)
    q_new = jnp.transpose(qn.reshape(2, R, KVW), (2, 0, 1))
    return err[None], q_new


def solution(mesh):
    return jax.shard_map(
        per_device,
        mesh=mesh,
        in_specs=(P("dp", "mp"), P("dp", None), P("dp", "mp", None), P()),
        out_specs=(P("dp", "mp", None), P()),
        check_vma=False,
    )
```

```python
import functools

import jax
import jax.numpy as jnp
from jax import lax
from jax.experimental import pallas as pl
from jax.experimental.pallas import tpu as pltpu
from jax.sharding import PartitionSpec as P

MESH = pl.DeviceIdType.MESH
F32 = jnp.float32
BF16 = jnp.bfloat16
HIGHEST = lax.Precision.HIGHEST

NY, NZ, NX, NC = 4, 8, 4, 2
TOK, ROWS, KVW, R = 1440, 1024, 1024, 32
TOK_PAD = 1536
WIDTH = 2 * KVW
CB = 8
CL = 128
N_PEERS = 31


def ring(step, size):
    return min(step, size - step)


DP_PEERS = sorted(
    [(a, b) for a in range(NY) for b in range(NZ) if (a, b) != (0, 0)],
    key=lambda o: -(ring(o[0], NY) + ring(o[1], NZ)),
)
BLOCK_PEERS = sorted(
    [(a, b, c) for a in range(NY) for b in range(NX) for c in range(NC) if (a, b, c) != (0, 0, 0)],
    key=lambda o: -(ring(o[0], NY) + ring(o[1], NX)),
)
Z_PEERS = sorted(range(1, NZ), key=lambda o: -ring(o, NZ))
MP_PEERS = sorted(
    [(b, c) for b in range(NX) for c in range(NC) if (b, c) != (0, 0)],
    key=lambda o: -ring(o[0], NX),
)


def split3(x):
    hi = x.astype(BF16)
    rest = x - hi.astype(F32)
    mid = rest.astype(BF16)
    low = (rest - mid.astype(F32)).astype(BF16)
    return hi, mid, low


def stack3(x):
    return jnp.concatenate(split3(x), axis=0)


def sum3(x):
    n = x.shape[0] // 3
    return x[:n] + (x[n : 2 * n] + x[2 * n :])


def dot(a, b, ca, cb):
    return lax.dot_general(a, b, (((ca,), (cb,)), ((), ())), preferred_element_type=F32)


def dot_high(a, b, ca, cb):
    return lax.dot_general(
        a, b, (((ca,), (cb,)), ((), ())), precision=HIGHEST, preferred_element_type=F32
    )


def chunk(index):
    row = pl.multiple_of((index // 8) * CB, CB)
    lane = pl.multiple_of(lax.rem(index, 8) * CL, CL)
    return pl.ds(row, CB), pl.ds(lane, CL)


def inverse_factors(gram):
    lane = lax.broadcasted_iota(jnp.int32, (R, 128), 1)
    row = lax.broadcasted_iota(jnp.int32, (R, 128), 0)
    first = lax.rem(lane // R, 2) == 0
    unit = jnp.where(lax.rem(lane, R) == row, 1.0, 0.0).astype(F32)
    w = jnp.where(lane < 2 * R, gram, unit)
    for k in range(R - 1):
        pivot_row = w[k : k + 1, :]
        f0 = w[:, k : k + 1] / pivot_row[:, k : k + 1]
        f1 = w[:, R + k : R + k + 1] / pivot_row[:, R + k : R + k + 1]
        factor = jnp.where(first, f0, f1)
        w = w - jnp.where(row > k, factor * pivot_row, 0.0)
    on0 = jnp.sum(jnp.where(lane == row, w, 0.0), axis=1, keepdims=True)
    on1 = jnp.sum(jnp.where(lane == row + R, w, 0.0), axis=1, keepdims=True)
    w = w * jnp.where(first, 1.0 / jnp.sqrt(on0), 1.0 / jnp.sqrt(on1))
    return w[:, 2 * R : 3 * R], w[:, 3 * R : 4 * R]


def exchange(
    a_hbm, g_hbm, f_hbm, qt_hbm, mat, phat, q_full, inv,
    a, g, f, qt, at, mhi, mlo, p_part, p_recv, p_full,
    gram_own, gram_recv, q_part, q_recv, z_recv,
    load_sem, send_sem, recv_sem,
):
    dp, mp = lax.axis_index("dp"), lax.axis_index("mp")
    y, z, x, c = dp // NZ, lax.rem(dp, NZ), mp // NC, lax.rem(mp, NC)
    block_id = y * 8 + mp

    def dp_target(o):
        return (lax.rem(y + o[0], NY) * NZ + lax.rem(z + o[1], NZ), mp)

    def block_target(o):
        return (
            lax.rem(y + o[0], NY) * NZ + z,
            lax.rem(x + o[1], NX) * NC + lax.rem(c + o[2], NC),
        )

    def z_target(o):
        return (y * NZ + lax.rem(z + o, NZ), mp)

    barrier = pltpu.get_barrier_semaphore()
    greeted = [dp_target(o) for o in DP_PEERS]
    greeted += [block_target(o) for o in BLOCK_PEERS if o[1:] != (0, 0)]
    for target in greeted:
        pl.semaphore_signal(barrier, inc=1, device_id=target, device_id_type=MESH)

    half = [pl.ds(m * KVW, KVW) for m in range(2)]
    loads = {}

    def load(name, src, dst):
        loads[name] = pltpu.make_async_copy(src, dst, load_sem.at[len(loads)])
        loads[name].start()

    load("q", qt_hbm, qt)
    load("g0", g_hbm.at[:, half[0]], g.at[pl.ds(0, TOK), half[0]])
    load("a", a_hbm, a.at[pl.ds(0, TOK), :])
    load("f0", f_hbm.at[:, half[0]], f.at[:, half[0]])
    load("g1", g_hbm.at[:, half[1]], g.at[pl.ds(0, TOK), half[1]])
    load("f1", f_hbm.at[:, half[1]], f.at[:, half[1]])
    g[TOK:, :] = jnp.zeros((TOK_PAD - TOK, WIDTH), BF16)
    a[TOK:, :] = jnp.zeros((TOK_PAD - TOK, ROWS), BF16)

    def send(src, dst, target, which):
        pltpu.make_async_remote_copy(
            src_ref=src,
            dst_ref=dst,
            send_sem=send_sem.at[which],
            recv_sem=recv_sem.at[which],
            device_id=target,
            device_id_type=MESH,
        ).start()

    def wait_on(sem, view):
        pltpu.make_async_copy(view, view, sem).wait()

    loads["q"].wait()
    for m in range(2):
        q3 = stack3(qt[pl.ds(m * R, R), :])
        loads[f"g{m}"].wait()
        inner3 = stack3(sum3(dot(q3, g[:, m * KVW : (m + 1) * KVW], 1, 1)))
        if m == 0:
            loads["a"].wait()
        part = sum3(dot(inner3, a[...], 1, 0))
        loads[f"f{m}"].wait()
        p_part[m] = part + sum3(dot(q3, f[:, m * KVW : (m + 1) * KVW], 1, 1))
        if m == 0:
            pl.semaphore_wait(barrier, len(greeted))
        for i, o in enumerate(DP_PEERS):
            target = dp_target(o)
            row, lane = chunk(target[0])
            send(p_part.at[m, row, lane], p_recv.at[m, i], target, m)

    at[...] = a[...].T

    def columns(n):
        lanes = pl.ds(pl.multiple_of(n * 256, 256), 256)
        block = dot(at[...], g[:, lanes], 1, 0) + f[:, lanes].astype(F32)
        mat[:, lanes] = block
        hi = block.astype(BF16)
        mhi[:, lanes] = hi
        mlo[:, lanes] = (block - hi.astype(F32)).astype(BF16)

    row, lane = chunk(dp)
    for m, first, last in ((0, 0, 4), (1, 4, 5)):
        pl.loop(first, last)(columns)
        wait_on(recv_sem.at[m], p_recv.at[m])
        own = p_part[m, row, lane]
        for i in range(N_PEERS):
            own = own + p_recv[m, i]
        p_full[m, row, lane] = own * (1.0 / 32)
        mine = p_full.at[m, row, lane]
        for o in DP_PEERS:
            send(mine, mine, dp_target(o), 2 + m)
    pl.loop(5, 8)(columns)

    for m in range(2):
        wait_on(recv_sem.at[2 + m], p_recv.at[m])
        cols = slice(m * KVW, (m + 1) * KVW)
        p3 = stack3(p_full[m])
        q_part[m] = sum3(dot(p3, mhi[:, cols], 1, 0) + dot(p3, mlo[:, cols], 1, 0))
        for i, o in enumerate(BLOCK_PEERS):
            target = block_target(o)
            r, l = chunk((target[0] // NZ) * 8 + target[1])
            send(q_part.at[m, r, l], q_recv.at[m, i], target, 4 + m)

    lane64 = lax.broadcasted_iota(jnp.int32, (R, 2 * R), 1)
    p_all = jnp.concatenate([p_full[0], p_full[1]], axis=0)
    both = dot_high(p_all, p_all, 1, 1)
    terms = jnp.where(lane64 < R, both[:R], both[R:])
    gram_own[...] = jnp.concatenate([terms, jnp.zeros((R, 128 - 2 * R), F32)], axis=1)
    for o in MP_PEERS:
        send(gram_own, gram_recv.at[mp], block_target((0,) + o), 10)
    gram_recv[mp] = gram_own[...]

    row, lane = chunk(block_id)
    for m in range(2):
        wait_on(recv_sem.at[4 + m], q_recv.at[m])
        own = q_part[m, row, lane]
        for i in range(N_PEERS):
            own = own + q_recv[m, i]
        z_recv[m, z] = own
        for o in Z_PEERS:
            send(z_recv.at[m, z], z_recv.at[m, z], z_target(o), 6 + m)

    wait_on(recv_sem.at[10], gram_recv.at[pl.ds(0, 7)])
    gram = gram_recv[0]
    for i in range(1, 8):
        gram = gram + gram_recv[i]
    inverses = inverse_factors(gram)

    for m in range(2):
        wait_on(recv_sem.at[6 + m], z_recv.at[m, pl.ds(0, 7)])
        own = z_recv[m, 0]
        for i in range(1, NZ):
            own = own + z_recv[m, i]
        q_full[m, row, lane] = own * (1.0 / 32)
        mine = q_full.at[m, row, lane]
        for o in BLOCK_PEERS:
            send(mine, mine, block_target(o), 8 + m)

    for m in range(2):
        inv[m] = inverses[m]
        hi, low, _ = split3(dot_high(inverses[m], p_full[m], 1, 0))
        phat[m] = jnp.concatenate([hi, low, hi, jnp.zeros_like(hi)], axis=0).T

    for m in range(2):
        wait_on(recv_sem.at[8 + m], q_recv.at[m])

    for m in range(2):
        wait_on(send_sem.at[m], p_recv.at[m])
        wait_on(send_sem.at[2 + m], p_recv.at[m])
        wait_on(send_sem.at[4 + m], q_recv.at[m])
        wait_on(send_sem.at[6 + m], z_recv.at[m, pl.ds(0, 7)])
        wait_on(send_sem.at[8 + m], q_recv.at[m])
    wait_on(send_sem.at[10], gram_recv.at[pl.ds(0, 7)])


def finish(mat, phat, q_full, inv, err_hbm, qn_hbm, err, qn, out_sem):
    laid = []
    for m in range(2):
        q_new = dot_high(inv[m], q_full[m], 1, 0)
        qn[pl.ds(m * R, R), :] = q_new
        hi, low, _ = split3(q_new)
        laid.append(jnp.concatenate([hi, hi, low, jnp.zeros_like(hi)], axis=0))
    outs = [pltpu.make_async_copy(qn, qn_hbm, out_sem.at[8])]
    outs[0].start()
    for i in range(8):
        rows = pl.ds(i * 128, 128)
        for m in range(2):
            cols = slice(m * KVW, (m + 1) * KVW)
            rebuilt = dot(phat[m, rows, :], laid[m], 1, 0)
            err[rows, cols] = (mat[rows, cols] - rebuilt).astype(BF16)
        copy = pltpu.make_async_copy(err.at[rows, :], err_hbm.at[rows, :], out_sem.at[i])
        copy.start()
        outs.append(copy)
    for copy in outs:
        copy.wait()


def per_device(activations, out_grads, feedback, q_prev):
    qt = jnp.transpose(q_prev, (1, 2, 0)).reshape(2 * R, KVW)
    any_space = pl.BlockSpec(memory_space=pl.ANY)
    vmem = pl.BlockSpec(memory_space=pltpu.VMEM)
    held = pl.pallas_call(
        exchange,
        out_shape=(
            pltpu.VMEM((ROWS, WIDTH), F32),
            pltpu.VMEM((2, ROWS, 128), BF16),
            pltpu.VMEM((2, R, KVW), F32),
            pltpu.VMEM((2, R, R), F32),
        ),
        in_specs=[any_space] * 4,
        out_specs=(vmem,) * 4,
        scratch_shapes=[
            pltpu.VMEM((TOK_PAD, ROWS), BF16),
            pltpu.VMEM((TOK_PAD, WIDTH), BF16),
            pltpu.VMEM((ROWS, WIDTH), BF16),
            pltpu.VMEM((2 * R, KVW), F32),
            pltpu.VMEM((ROWS, TOK_PAD), BF16),
            pltpu.VMEM((ROWS, WIDTH), BF16),
            pltpu.VMEM((ROWS, WIDTH), BF16),
            pltpu.VMEM((2, R, ROWS), F32),
            pltpu.VMEM((2, N_PEERS, CB, CL), F32),
            pltpu.VMEM((2, R, ROWS), F32),
            pltpu.VMEM((R, 128), F32),
            pltpu.VMEM((8, R, 128), F32),
            pltpu.VMEM((2, R, KVW), F32),
            pltpu.VMEM((2, N_PEERS, CB, CL), F32),
            pltpu.VMEM((2, NZ, CB, CL), F32),
            pltpu.SemaphoreType.DMA((6,)),
            pltpu.SemaphoreType.DMA((11,)),
            pltpu.SemaphoreType.DMA((11,)),
        ],
        compiler_params=pltpu.CompilerParams(
            collective_id=0, has_side_effects=True, vmem_limit_bytes=40 * 2**20
        ),
    )(*[pltpu.with_memory_space_constraint(v, pltpu.HBM) for v in (activations, out_grads, feedback[0], qt)])
    err, qn = pl.pallas_call(
        finish,
        out_shape=(
            jax.ShapeDtypeStruct((ROWS, WIDTH), BF16),
            jax.ShapeDtypeStruct((2 * R, KVW), F32),
        ),
        in_specs=[vmem] * 4,
        out_specs=(any_space,) * 2,
        scratch_shapes=[
            pltpu.VMEM((ROWS, WIDTH), BF16),
            pltpu.VMEM((2 * R, KVW), F32),
            pltpu.SemaphoreType.DMA((9,)),
        ],
        compiler_params=pltpu.CompilerParams(vmem_limit_bytes=24 * 2**20),
    )(*held)
    q_new = jnp.transpose(qn.reshape(2, R, KVW), (2, 0, 1))
    return err[None], q_new


def solution(mesh):
    return jax.shard_map(
        per_device,
        mesh=mesh,
        in_specs=(P("dp", "mp"), P("dp", None), P("dp", "mp", None), P()),
        out_specs=(P("dp", "mp", None), P()),
        check_vma=False,
    )
```

```python
import functools

import jax
import jax.numpy as jnp
from jax import lax
from jax.experimental import pallas as pl
from jax.experimental.pallas import tpu as pltpu
from jax.sharding import PartitionSpec as P

MESH = pl.DeviceIdType.MESH
F32 = jnp.float32
BF16 = jnp.bfloat16
HIGHEST = lax.Precision.HIGHEST

NY, NZ, NX, NC = 4, 8, 4, 2
TOK, ROWS, KVW, R = 1440, 1024, 1024, 32
TOK_PAD = 1536
WIDTH = 2 * KVW
CB = 8
CL = 128
N_PEERS = 31


def ring(step, size):
    return min(step, size - step)


DP_PEERS = sorted(
    [(a, b) for a in range(NY) for b in range(NZ) if (a, b) != (0, 0)],
    key=lambda o: -(ring(o[0], NY) + ring(o[1], NZ)),
)
BLOCK_PEERS = sorted(
    [(a, b, c) for a in range(NY) for b in range(NX) for c in range(NC) if (a, b, c) != (0, 0, 0)],
    key=lambda o: -(ring(o[0], NY) + ring(o[1], NX)),
)
FAR_Y = (2, 1, 3, 0)
Z_PEERS = sorted(range(1, NZ), key=lambda o: -ring(o, NZ))
MP_PEERS = sorted(
    [(b, c) for b in range(NX) for c in range(NC) if (b, c) != (0, 0)],
    key=lambda o: -ring(o[0], NX),
)


def split3(x):
    hi = x.astype(BF16)
    rest = x - hi.astype(F32)
    mid = rest.astype(BF16)
    low = (rest - mid.astype(F32)).astype(BF16)
    return hi, mid, low


def stack3(x):
    return jnp.concatenate(split3(x), axis=0)


def lay(x, order):
    parts = split3(x)
    return jnp.concatenate([parts[i] for i in order] + [jnp.zeros_like(parts[0])] * 2, axis=0)


LEFT_PARTS = (0, 0, 1, 1, 0, 2)
RIGHT_PARTS = (0, 1, 0, 1, 2, 0)


def sum3(x):
    n = x.shape[0] // 3
    return x[:n] + (x[n : 2 * n] + x[2 * n :])


def dot(a, b, ca, cb):
    return lax.dot_general(a, b, (((ca,), (cb,)), ((), ())), preferred_element_type=F32)


def dot_high(a, b, ca, cb):
    return lax.dot_general(
        a, b, (((ca,), (cb,)), ((), ())), precision=HIGHEST, preferred_element_type=F32
    )


def chunk(index):
    row = pl.multiple_of((index // 8) * CB, CB)
    lane = pl.multiple_of(lax.rem(index, 8) * CL, CL)
    return pl.ds(row, CB), pl.ds(lane, CL)


def inverse_factors(gram):
    lane = lax.broadcasted_iota(jnp.int32, (R, 128), 1)
    row = lax.broadcasted_iota(jnp.int32, (R, 128), 0)
    first = lax.rem(lane // R, 2) == 0
    unit = jnp.where(lax.rem(lane, R) == row, 1.0, 0.0).astype(F32)
    w = jnp.where(lane < 2 * R, gram, unit)
    for k in range(R - 1):
        pivot_row = w[k : k + 1, :]
        f0 = w[:, k : k + 1] / pivot_row[:, k : k + 1]
        f1 = w[:, R + k : R + k + 1] / pivot_row[:, R + k : R + k + 1]
        factor = jnp.where(first, f0, f1)
        w = w - jnp.where(row > k, factor * pivot_row, 0.0)
    on0 = jnp.sum(jnp.where(lane == row, w, 0.0), axis=1, keepdims=True)
    on1 = jnp.sum(jnp.where(lane == row + R, w, 0.0), axis=1, keepdims=True)
    w = w * jnp.where(first, 1.0 / jnp.sqrt(on0), 1.0 / jnp.sqrt(on1))
    return w[:, 2 * R : 3 * R], w[:, 3 * R : 4 * R]


def exchange(
    a_hbm, g_hbm, f_hbm, qt_hbm, err0, qn0, mat1, left1, q_full, inv1,
    a, g, f, qt, at, mat0, left0, mhi, mlo, p_part, p_recv, p_full,
    gram_own, gram_recv, q_part, q_recv, z_recv,
    load_sem, send_sem, recv_sem,
):
    dp, mp = lax.axis_index("dp"), lax.axis_index("mp")
    y, z, x, c = dp // NZ, lax.rem(dp, NZ), mp // NC, lax.rem(mp, NC)
    block_id = y * 8 + mp

    def dp_target(o):
        return (lax.rem(y + o[0], NY) * NZ + lax.rem(z + o[1], NZ), mp)

    def block_target(o):
        return (
            lax.rem(y + o[0], NY) * NZ + z,
            lax.rem(x + o[1], NX) * NC + lax.rem(c + o[2], NC),
        )

    def z_target(o):
        return (y * NZ + lax.rem(z + o, NZ), mp)

    barrier = pltpu.get_barrier_semaphore()
    greeted = [dp_target(o) for o in DP_PEERS]
    greeted += [block_target(o) for o in BLOCK_PEERS if o[1:] != (0, 0)]
    for target in greeted:
        pl.semaphore_signal(barrier, inc=1, device_id=target, device_id_type=MESH)

    half = [pl.ds(m * KVW, KVW) for m in range(2)]
    loads = {}

    def load(name, src, dst):
        loads[name] = pltpu.make_async_copy(src, dst, load_sem.at[len(loads)])
        loads[name].start()

    load("q", qt_hbm, qt)
    for m in range(2):
        load(f"g{m}", g_hbm.at[:, half[m]], g.at[pl.ds(0, TOK), half[m]])
        if m == 0:
            load("a", a_hbm, a.at[pl.ds(0, TOK), :])
        load(f"f{m}", f_hbm.at[:, half[m]], f.at[:, half[m]])
    g[TOK:, :] = jnp.zeros((TOK_PAD - TOK, WIDTH), BF16)
    a[TOK:, :] = jnp.zeros((TOK_PAD - TOK, ROWS), BF16)

    def arrival(dz, m):
        opposite = lax.rem(lax.rem(z + dz, NZ) // 2 + 2, 4) == z // 2
        return jnp.where(opposite, 11 + m, 2 + m)

    def send(src, dst, target, which, arrives=None):
        pltpu.make_async_remote_copy(
            src_ref=src,
            dst_ref=dst,
            send_sem=send_sem.at[which],
            recv_sem=recv_sem.at[which if arrives is None else arrives],
            device_id=target,
            device_id_type=MESH,
        ).start()

    def wait_on(sem, view):
        pltpu.make_async_copy(view, view, sem).wait()

    loads["q"].wait()
    for m in range(2):
        cols = slice(m * KVW, (m + 1) * KVW)
        q3 = stack3(qt[pl.ds(m * R, R), :])
        loads[f"g{m}"].wait()
        inner3 = stack3(sum3(dot(q3, g[:, cols], 1, 1)))
        if m == 0:
            loads["a"].wait()
        loads[f"f{m}"].wait()
        if m == 0:
            pl.semaphore_wait(barrier, len(greeted))
        part = sum3(dot(inner3, a[...], 1, 0))
        p_part[m] = part + sum3(dot(q3, f[:, cols], 1, 1))
        for i, o in enumerate(DP_PEERS):
            target = dp_target(o)
            row, lane = chunk(target[0])
            send(p_part.at[m, row, lane], p_recv.at[m, i], target, m)

    at[...] = a[...].T

    def columns(n):
        m, lanes = n // 2, slice(n * 512, (n + 1) * 512)
        block = dot(at[...], g[:, lanes], 1, 0) + f[:, lanes].astype(F32)
        (mat0, mat1)[m][:, (n % 2) * 512 : (n % 2 + 1) * 512] = block
        hi = block.astype(BF16)
        mhi[:, lanes] = hi
        mlo[:, lanes] = (block - hi.astype(F32)).astype(BF16)

    row, lane = chunk(dp)
    for m in range(2):
        columns(m)
        wait_on(recv_sem.at[m], p_recv.at[m])
        own = p_part[m, row, lane]
        for i in range(N_PEERS):
            own = own + p_recv[m, i]
        p_full[m, row, lane] = own * (1.0 / 32)
        mine = p_full.at[m, row, lane]
        for o in DP_PEERS:
            send(mine, mine, dp_target(o), 2 + m, arrival(o[1], m))
    columns(2)
    columns(3)

    for m in range(2):
        terms = []
        for step in (1, 3, 0, 2):
            if step == 1:
                wait_on(recv_sem.at[2 + m], p_recv.at[m, pl.ds(0, N_PEERS - 8)])
            if step == 2:
                wait_on(recv_sem.at[11 + m], p_recv.at[m, pl.ds(0, 8)])
            pair = lax.rem(z // 2 + step, 4)
            wide = pl.ds(pl.multiple_of(pair * 256, 256), 256)
            cols = slice(m * KVW, (m + 1) * KVW)
            p3 = stack3(p_full[m, :, wide])
            terms.append(dot(p3, mhi[wide, cols], 1, 0) + dot(p3, mlo[wide, cols], 1, 0))
        q_part[m] = sum3(terms[0] + terms[1] + terms[2] + terms[3])
        for i, o in enumerate(BLOCK_PEERS):
            target = block_target(o)
            r, l = chunk((target[0] // NZ) * 8 + target[1])
            send(q_part.at[m, r, l], q_recv.at[m, i], target, 4 + m)

    lane64 = lax.broadcasted_iota(jnp.int32, (R, 2 * R), 1)
    p_all = jnp.concatenate([p_full[0], p_full[1]], axis=0)
    both = dot_high(p_all, p_all, 1, 1)
    terms = jnp.where(lane64 < R, both[:R], both[R:])
    gram_own[...] = jnp.concatenate([terms, jnp.zeros((R, 128 - 2 * R), F32)], axis=1)
    for o in MP_PEERS:
        send(gram_own, gram_recv.at[mp], block_target((0,) + o), 10)
    gram_recv[mp] = gram_own[...]

    row, lane = chunk(block_id)
    for m in range(2):
        wait_on(recv_sem.at[4 + m], q_recv.at[m])
        own = q_part[m, row, lane]
        for i in range(N_PEERS):
            own = own + q_recv[m, i]
        z_recv[m, z] = own
        for o in Z_PEERS:
            send(z_recv.at[m, z], z_recv.at[m, z], z_target(o), 6 + m)

    wait_on(recv_sem.at[10], gram_recv.at[pl.ds(0, 7)])
    gram = gram_recv[0]
    for i in range(1, 8):
        gram = gram + gram_recv[i]
    inverses = inverse_factors(gram)

    for m in range(2):
        wait_on(recv_sem.at[6 + m], z_recv.at[m, pl.ds(0, 7)])
        own = z_recv[m, 0]
        for i in range(1, NZ):
            own = own + z_recv[m, i]
        q_full[m, row, lane] = own * (1.0 / 32)
        mine = q_full.at[m, row, lane]
        for o in BLOCK_PEERS:
            send(mine, mine, block_target(o), 8 + m)

    inv1[...] = inverses[1]
    for m in range(2):
        normed = dot_high(inverses[m], p_full[m], 1, 0)
        left = dot_high(inverses[m], normed, 0, 0)
        (left0, left1)[m][...] = lay(left, LEFT_PARTS).T

    wait_on(recv_sem.at[8], q_recv.at[0])
    raw = q_full[0]
    laid = lay(raw, RIGHT_PARTS)
    for i in range(4):
        rows = pl.ds(i * 256, 256)
        err0[rows, :] = (mat0[rows, :] - dot(left0[rows, :], laid, 1, 0)).astype(BF16)
    qn0[...] = dot_high(inverses[0], raw, 1, 0)
    wait_on(recv_sem.at[9], q_recv.at[1])

    for m in range(2):
        wait_on(send_sem.at[m], p_recv.at[m])
        wait_on(send_sem.at[2 + m], p_recv.at[m])
        wait_on(send_sem.at[4 + m], q_recv.at[m])
        wait_on(send_sem.at[6 + m], z_recv.at[m, pl.ds(0, 7)])
        wait_on(send_sem.at[8 + m], q_recv.at[m])
    wait_on(send_sem.at[10], gram_recv.at[pl.ds(0, 7)])


def finish(err0, qn0, mat1, left1, q_full, inv1, err_hbm, qn_hbm, err1, qn1, out_sem):
    outs = []

    def store(src, dst):
        outs.append(pltpu.make_async_copy(src, dst, out_sem.at[len(outs)]))
        outs[-1].start()

    store(err0, err_hbm.at[:, pl.ds(0, KVW)])
    store(qn0, qn_hbm.at[pl.ds(0, R), :])
    raw = q_full[1]
    laid = lay(raw, RIGHT_PARTS)
    for i in range(4):
        rows = pl.ds(i * 256, 256)
        err1[rows, :] = (mat1[rows, :] - dot(left1[rows, :], laid, 1, 0)).astype(BF16)
        store(err1.at[rows, :], err_hbm.at[rows, pl.ds(KVW, KVW)])
    qn1[...] = dot_high(inv1[...], raw, 1, 0)
    store(qn1, qn_hbm.at[pl.ds(R, R), :])
    for copy in outs:
        copy.wait()


def per_device(activations, out_grads, feedback, q_prev):
    qt = jnp.transpose(q_prev, (1, 2, 0)).reshape(2 * R, KVW)
    any_space = pl.BlockSpec(memory_space=pl.ANY)
    vmem = pl.BlockSpec(memory_space=pltpu.VMEM)
    held = pl.pallas_call(
        exchange,
        out_shape=(
            pltpu.VMEM((ROWS, KVW), BF16),
            pltpu.VMEM((R, KVW), F32),
            pltpu.VMEM((ROWS, KVW), F32),
            pltpu.VMEM((ROWS, 256), BF16),
            pltpu.VMEM((2, R, KVW), F32),
            pltpu.VMEM((R, R), F32),
        ),
        in_specs=[any_space] * 4,
        out_specs=(vmem,) * 6,
        scratch_shapes=[
            pltpu.VMEM((TOK_PAD, ROWS), BF16),
            pltpu.VMEM((TOK_PAD, WIDTH), BF16),
            pltpu.VMEM((ROWS, WIDTH), BF16),
            pltpu.VMEM((2 * R, KVW), F32),
            pltpu.VMEM((ROWS, TOK_PAD), BF16),
            pltpu.VMEM((ROWS, KVW), F32),
            pltpu.VMEM((ROWS, 256), BF16),
            pltpu.VMEM((ROWS, WIDTH), BF16),
            pltpu.VMEM((ROWS, WIDTH), BF16),
            pltpu.VMEM((2, R, ROWS), F32),
            pltpu.VMEM((2, N_PEERS, CB, CL), F32),
            pltpu.VMEM((2, R, ROWS), F32),
            pltpu.VMEM((R, 128), F32),
            pltpu.VMEM((8, R, 128), F32),
            pltpu.VMEM((2, R, KVW), F32),
            pltpu.VMEM((2, N_PEERS, CB, CL), F32),
            pltpu.VMEM((2, NZ, CB, CL), F32),
            pltpu.SemaphoreType.DMA((10,)),
            pltpu.SemaphoreType.DMA((11,)),
            pltpu.SemaphoreType.DMA((13,)),
        ],
        compiler_params=pltpu.CompilerParams(
            collective_id=0, has_side_effects=True, vmem_limit_bytes=40 * 2**20
        ),
    )(*[pltpu.with_memory_space_constraint(v, pltpu.HBM) for v in (activations, out_grads, feedback[0], qt)])
    err, qn = pl.pallas_call(
        finish,
        out_shape=(
            jax.ShapeDtypeStruct((ROWS, WIDTH), BF16),
            jax.ShapeDtypeStruct((2 * R, KVW), F32),
        ),
        in_specs=[vmem] * 6,
        out_specs=(any_space,) * 2,
        scratch_shapes=[
            pltpu.VMEM((ROWS, KVW), BF16),
            pltpu.VMEM((R, KVW), F32),
            pltpu.SemaphoreType.DMA((7,)),
        ],
        compiler_params=pltpu.CompilerParams(vmem_limit_bytes=24 * 2**20),
    )(*held)
    q_new = jnp.transpose(qn.reshape(2, R, KVW), (2, 0, 1))
    return err[None], q_new


def solution(mesh):
    return jax.shard_map(
        per_device,
        mesh=mesh,
        in_specs=(P("dp", "mp"), P("dp", None), P("dp", "mp", None), P()),
        out_specs=(P("dp", "mp", None), P()),
        check_vma=False,
    )
```

```python
import functools

import jax
import jax.numpy as jnp
from jax import lax
from jax.experimental import pallas as pl
from jax.experimental.pallas import tpu as pltpu
from jax.sharding import PartitionSpec as P

MESH = pl.DeviceIdType.MESH
F32 = jnp.float32
BF16 = jnp.bfloat16
HIGHEST = lax.Precision.HIGHEST

NY, NZ, NX, NC = 4, 8, 4, 2
TOK, ROWS, KVW, R = 1440, 1024, 1024, 32
TOK_PAD = 1536
WIDTH = 2 * KVW
CB = 8
CL = 128
N_PEERS = 31


def ring(step, size):
    return min(step, size - step)


DP_PEERS = sorted(
    [(a, b) for a in range(NY) for b in range(NZ) if (a, b) != (0, 0)],
    key=lambda o: -(ring(o[0], NY) + ring(o[1], NZ)),
)
BLOCK_PEERS = sorted(
    [(a, b, c) for a in range(NY) for b in range(NX) for c in range(NC) if (a, b, c) != (0, 0, 0)],
    key=lambda o: -(ring(o[0], NY) + ring(o[1], NX)),
)
FAR_Y = (2, 1, 3, 0)
Z_PEERS = sorted(range(1, NZ), key=lambda o: -ring(o, NZ))
MP_PEERS = sorted(
    [(b, c) for b in range(NX) for c in range(NC) if (b, c) != (0, 0)],
    key=lambda o: -ring(o[0], NX),
)


def split3(x):
    hi = x.astype(BF16)
    rest = x - hi.astype(F32)
    mid = rest.astype(BF16)
    low = (rest - mid.astype(F32)).astype(BF16)
    return hi, mid, low


def stack3(x):
    return jnp.concatenate(split3(x), axis=0)


def lay(x, order):
    parts = split3(x)
    return jnp.concatenate([parts[i] for i in order] + [jnp.zeros_like(parts[0])] * 2, axis=0)


LEFT_PARTS = (0, 0, 1, 1, 0, 2)
RIGHT_PARTS = (0, 1, 0, 1, 2, 0)
ERR0_CUTS = 4


def sum3(x):
    n = x.shape[0] // 3
    return x[:n] + (x[n : 2 * n] + x[2 * n :])


def dot(a, b, ca, cb):
    return lax.dot_general(a, b, (((ca,), (cb,)), ((), ())), preferred_element_type=F32)


def dot_high(a, b, ca, cb):
    return lax.dot_general(
        a, b, (((ca,), (cb,)), ((), ())), precision=HIGHEST, preferred_element_type=F32
    )


def chunk(index):
    row = pl.multiple_of((index // 8) * CB, CB)
    lane = pl.multiple_of(lax.rem(index, 8) * CL, CL)
    return pl.ds(row, CB), pl.ds(lane, CL)


def inverse_factors(gram):
    lane = lax.broadcasted_iota(jnp.int32, (R, 128), 1)
    row = lax.broadcasted_iota(jnp.int32, (R, 128), 0)
    first = lax.rem(lane // R, 2) == 0
    unit = jnp.where(lax.rem(lane, R) == row, 1.0, 0.0).astype(F32)
    w = jnp.where(lane < 2 * R, gram, unit)
    for k in range(R - 1):
        pivot_row = w[k : k + 1, :]
        f0 = w[:, k : k + 1] / pivot_row[:, k : k + 1]
        f1 = w[:, R + k : R + k + 1] / pivot_row[:, R + k : R + k + 1]
        factor = jnp.where(first, f0, f1)
        w = w - jnp.where(row > k, factor * pivot_row, 0.0)
    on0 = jnp.sum(jnp.where(lane == row, w, 0.0), axis=1, keepdims=True)
    on1 = jnp.sum(jnp.where(lane == row + R, w, 0.0), axis=1, keepdims=True)
    w = w * jnp.where(first, 1.0 / jnp.sqrt(on0), 1.0 / jnp.sqrt(on1))
    return w[:, 2 * R : 3 * R], w[:, 3 * R : 4 * R]


def exchange(
    a_hbm, g_hbm, f_hbm, qt_hbm, err0, mat1, left1, q_full, inv,
    a, g, f, qt, at, mat0, left0, mhi, mlo, p_part, p_recv, p_full,
    gram_own, gram_recv, q_part, q_recv, z_recv,
    load_sem, send_sem, recv_sem,
):
    dp, mp = lax.axis_index("dp"), lax.axis_index("mp")
    y, z, x, c = dp // NZ, lax.rem(dp, NZ), mp // NC, lax.rem(mp, NC)
    block_id = y * 8 + mp

    def dp_target(o):
        return (lax.rem(y + o[0], NY) * NZ + lax.rem(z + o[1], NZ), mp)

    def block_target(o):
        return (
            lax.rem(y + o[0], NY) * NZ + z,
            lax.rem(x + o[1], NX) * NC + lax.rem(c + o[2], NC),
        )

    def z_target(o):
        return (y * NZ + lax.rem(z + o, NZ), mp)

    half = [pl.ds(m * KVW, KVW) for m in range(2)]
    loads = {}

    def load(name, src, dst):
        loads[name] = pltpu.make_async_copy(src, dst, load_sem.at[len(loads)])
        loads[name].start()

    load("q", qt_hbm, qt)
    for m in range(2):
        load(f"g{m}", g_hbm.at[:, half[m]], g.at[pl.ds(0, TOK), half[m]])
        if m == 0:
            load("a", a_hbm, a.at[pl.ds(0, TOK), :])
        load(f"f{m}", f_hbm.at[:, half[m]], f.at[:, half[m]])
    barrier = pltpu.get_barrier_semaphore()
    greeted = [dp_target(o) for o in DP_PEERS]
    greeted += [block_target(o) for o in BLOCK_PEERS if o[1:] != (0, 0)]
    for target in greeted:
        pl.semaphore_signal(barrier, inc=1, device_id=target, device_id_type=MESH)

    g[TOK:, :] = jnp.zeros((TOK_PAD - TOK, WIDTH), BF16)
    a[TOK:, :] = jnp.zeros((TOK_PAD - TOK, ROWS), BF16)

    def arrival(dz, m):
        opposite = lax.rem(lax.rem(z + dz, NZ) // 2 + 2, 4) == z // 2
        return jnp.where(opposite, 11 + m, 2 + m)

    def send(src, dst, target, which, arrives=None):
        pltpu.make_async_remote_copy(
            src_ref=src,
            dst_ref=dst,
            send_sem=send_sem.at[which],
            recv_sem=recv_sem.at[which if arrives is None else arrives],
            device_id=target,
            device_id_type=MESH,
        ).start()

    def wait_on(sem, view):
        pltpu.make_async_copy(view, view, sem).wait()

    def left_factors(m):
        cols = slice(m * KVW, (m + 1) * KVW)
        q3 = stack3(qt[pl.ds(m * R, R), :])
        loads[f"g{m}"].wait()
        inner3 = stack3(sum3(dot(q3, g[:, cols], 1, 1)))
        if m == 0:
            loads["a"].wait()
        part = sum3(dot(inner3, a[...], 1, 0))
        loads[f"f{m}"].wait()
        p_part[m] = part + sum3(dot(q3, f[:, cols], 1, 1))

    loads["q"].wait()
    for m in range(2):
        pl.when(dp >= 0)(functools.partial(left_factors, m))
        if m == 0:
            pl.semaphore_wait(barrier, len(greeted))
        for i, o in enumerate(DP_PEERS):
            target = dp_target(o)
            row, lane = chunk(target[0])
            send(p_part.at[m, row, lane], p_recv.at[m, i], target, m)

    at[...] = a[...].T

    def columns(n):
        m, lanes = n // 2, slice(n * 512, (n + 1) * 512)
        block = dot(at[...], g[:, lanes], 1, 0) + f[:, lanes].astype(F32)
        (mat0, mat1)[m][:, (n % 2) * 512 : (n % 2 + 1) * 512] = block
        hi = block.astype(BF16)
        mhi[:, lanes] = hi
        mlo[:, lanes] = (block - hi.astype(F32)).astype(BF16)

    row, lane = chunk(dp)
    for m in range(2):
        columns(m)
        wait_on(recv_sem.at[m], p_recv.at[m])
        own = p_part[m, row, lane]
        for i in range(N_PEERS):
            own = own + p_recv[m, i]
        p_full[m, row, lane] = own * (1.0 / 32)
        mine = p_full.at[m, row, lane]
        for o in DP_PEERS:
            send(mine, mine, dp_target(o), 2 + m, arrival(o[1], m))
    columns(2)
    columns(3)

    for m in range(2):
        terms = []
        for step in (1, 3, 0, 2):
            if step == 1:
                wait_on(recv_sem.at[2 + m], p_recv.at[m, pl.ds(0, N_PEERS - 8)])
            if step == 2:
                wait_on(recv_sem.at[11 + m], p_recv.at[m, pl.ds(0, 8)])
            pair = lax.rem(z // 2 + step, 4)
            wide = pl.ds(pl.multiple_of(pair * 256, 256), 256)
            cols = slice(m * KVW, (m + 1) * KVW)
            p3 = stack3(p_full[m, :, wide])
            terms.append(dot(p3, mhi[wide, cols], 1, 0) + dot(p3, mlo[wide, cols], 1, 0))
        q_part[m] = sum3(terms[0] + terms[1] + terms[2] + terms[3])
        for i, o in enumerate(BLOCK_PEERS):
            target = block_target(o)
            r, l = chunk((target[0] // NZ) * 8 + target[1])
            send(q_part.at[m, r, l], q_recv.at[m, i], target, 4 + m)

    lane64 = lax.broadcasted_iota(jnp.int32, (R, 2 * R), 1)
    p_all = jnp.concatenate([p_full[0], p_full[1]], axis=0)
    both = dot_high(p_all, p_all, 1, 1)
    terms = jnp.where(lane64 < R, both[:R], both[R:])
    gram_own[...] = jnp.concatenate([terms, jnp.zeros((R, 128 - 2 * R), F32)], axis=1)
    for o in MP_PEERS:
        send(gram_own, gram_recv.at[mp], block_target((0,) + o), 10)
    gram_recv[mp] = gram_own[...]

    row, lane = chunk(block_id)
    for m in range(2):
        wait_on(recv_sem.at[4 + m], q_recv.at[m])
        own = q_part[m, row, lane]
        for i in range(N_PEERS):
            own = own + q_recv[m, i]
        z_recv[m, z] = own
        for o in Z_PEERS:
            send(z_recv.at[m, z], z_recv.at[m, z], z_target(o), 6 + m)

    wait_on(recv_sem.at[10], gram_recv.at[pl.ds(0, 7)])
    gram = gram_recv[0]
    for i in range(1, 8):
        gram = gram + gram_recv[i]
    inverses = inverse_factors(gram)

    for m in range(2):
        wait_on(recv_sem.at[6 + m], z_recv.at[m, pl.ds(0, 7)])
        own = z_recv[m, 0]
        for i in range(1, NZ):
            own = own + z_recv[m, i]
        q_full[m, row, lane] = own * (1.0 / 32)
        mine = q_full.at[m, row, lane]
        for o in BLOCK_PEERS:
            send(mine, mine, block_target(o), 8 + m)

    for m in range(2):
        wait_on(send_sem.at[m], p_recv.at[m])
        wait_on(send_sem.at[2 + m], p_recv.at[m])
        wait_on(send_sem.at[4 + m], q_recv.at[m])
        wait_on(send_sem.at[6 + m], z_recv.at[m, pl.ds(0, 7)])
    wait_on(send_sem.at[10], gram_recv.at[pl.ds(0, 7)])

    inv[0] = inverses[0]
    inv[1] = inverses[1]
    for m in range(2):
        normed = dot_high(inverses[m], p_full[m], 1, 0)
        left = dot_high(inverses[m], normed, 0, 0)
        (left0, left1)[m][...] = lay(left, LEFT_PARTS).T

    wait_on(recv_sem.at[8], q_recv.at[0])
    raw = q_full[0]
    laid = lay(raw, RIGHT_PARTS)
    for i in range(4):
        rows = pl.ds(i * 256, 256)
        err0[rows, :] = (mat0[rows, :] - dot(left0[rows, :], laid, 1, 0)).astype(BF16)
    wait_on(recv_sem.at[9], q_recv.at[1])

    for m in range(2):
        wait_on(send_sem.at[8 + m], q_recv.at[m])


def finish(err0, mat1, left1, q_full, inv, err_hbm, qn_hbm, err1, qn, out_sem):
    outs = []

    def store(src, dst):
        outs.append(pltpu.make_async_copy(src, dst, out_sem.at[len(outs)]))
        outs[-1].start()

    for i in range(ERR0_CUTS):
        rows = pl.ds(i * (ROWS // ERR0_CUTS), ROWS // ERR0_CUTS)
        store(err0.at[rows, :], err_hbm.at[rows, pl.ds(0, KVW)])
    laid = lay(q_full[1], RIGHT_PARTS)
    for i in range(4):
        rows = pl.ds(i * 256, 256)
        err1[rows, :] = (mat1[rows, :] - dot(left1[rows, :], laid, 1, 0)).astype(BF16)
        store(err1.at[rows, :], err_hbm.at[rows, pl.ds(KVW, KVW)])
    for m in range(2):
        qn[pl.ds(m * R, R), :] = dot_high(inv[m], q_full[m], 1, 0)
    store(qn, qn_hbm)
    for copy in outs:
        copy.wait()


def per_device(activations, out_grads, feedback, q_prev):
    qt = jnp.transpose(q_prev, (1, 2, 0)).reshape(2 * R, KVW)
    any_space = pl.BlockSpec(memory_space=pl.ANY)
    vmem = pl.BlockSpec(memory_space=pltpu.VMEM)
    held = pl.pallas_call(
        exchange,
        out_shape=(
            pltpu.VMEM((ROWS, KVW), BF16),
            pltpu.VMEM((ROWS, KVW), F32),
            pltpu.VMEM((ROWS, 256), BF16),
            pltpu.VMEM((2, R, KVW), F32),
            pltpu.VMEM((2, R, R), F32),
        ),
        in_specs=[any_space] * 4,
        out_specs=(vmem,) * 5,
        scratch_shapes=[
            pltpu.VMEM((TOK_PAD, ROWS), BF16),
            pltpu.VMEM((TOK_PAD, WIDTH), BF16),
            pltpu.VMEM((ROWS, WIDTH), BF16),
            pltpu.VMEM((2 * R, KVW), F32),
            pltpu.VMEM((ROWS, TOK_PAD), BF16),
            pltpu.VMEM((ROWS, KVW), F32),
            pltpu.VMEM((ROWS, 256), BF16),
            pltpu.VMEM((ROWS, WIDTH), BF16),
            pltpu.VMEM((ROWS, WIDTH), BF16),
            pltpu.VMEM((2, R, ROWS), F32),
            pltpu.VMEM((2, N_PEERS, CB, CL), F32),
            pltpu.VMEM((2, R, ROWS), F32),
            pltpu.VMEM((R, 128), F32),
            pltpu.VMEM((8, R, 128), F32),
            pltpu.VMEM((2, R, KVW), F32),
            pltpu.VMEM((2, N_PEERS, CB, CL), F32),
            pltpu.VMEM((2, NZ, CB, CL), F32),
            pltpu.SemaphoreType.DMA((10,)),
            pltpu.SemaphoreType.DMA((11,)),
            pltpu.SemaphoreType.DMA((13,)),
        ],
        compiler_params=pltpu.CompilerParams(
            collective_id=0, has_side_effects=True, vmem_limit_bytes=40 * 2**20
        ),
    )(*[pltpu.with_memory_space_constraint(v, pltpu.HBM) for v in (activations, out_grads, feedback[0], qt)])
    err, qn = pl.pallas_call(
        finish,
        out_shape=(
            jax.ShapeDtypeStruct((ROWS, WIDTH), BF16),
            jax.ShapeDtypeStruct((2 * R, KVW), F32),
        ),
        in_specs=[vmem] * 5,
        out_specs=(any_space,) * 2,
        scratch_shapes=[
            pltpu.VMEM((ROWS, KVW), BF16),
            pltpu.VMEM((2 * R, KVW), F32),
            pltpu.SemaphoreType.DMA((ERR0_CUTS + 5,)),
        ],
        compiler_params=pltpu.CompilerParams(vmem_limit_bytes=24 * 2**20),
    )(*held)
    q_new = jnp.transpose(qn.reshape(2, R, KVW), (2, 0, 1))
    return err[None], q_new


def solution(mesh):
    return jax.shard_map(
        per_device,
        mesh=mesh,
        in_specs=(P("dp", "mp"), P("dp", None), P("dp", "mp", None), P()),
        out_specs=(P("dp", "mp", None), P()),
        check_vma=False,
    )
```

```python
import functools

import jax
import jax.numpy as jnp
from jax import lax
from jax.experimental import pallas as pl
from jax.experimental.pallas import tpu as pltpu
from jax.sharding import PartitionSpec as P

MESH = pl.DeviceIdType.MESH
F32 = jnp.float32
BF16 = jnp.bfloat16
HIGHEST = lax.Precision.HIGHEST

NY, NZ, NX, NC = 4, 8, 4, 2
TOK, ROWS, KVW, R = 1440, 1024, 1024, 32
TOK_PAD = 1536
WIDTH = 2 * KVW
CB = 8
CL = 128
N_PEERS = 31


def ring(step, size):
    return min(step, size - step)


DP_PEERS = sorted(
    [(a, b) for a in range(NY) for b in range(NZ) if (a, b) != (0, 0)],
    key=lambda o: -(ring(o[0], NY) + ring(o[1], NZ)),
)
BLOCK_PEERS = sorted(
    [(a, b, c) for a in range(NY) for b in range(NX) for c in range(NC) if (a, b, c) != (0, 0, 0)],
    key=lambda o: -(ring(o[0], NY) + ring(o[1], NX)),
)
FAR_Y = (2, 1, 3, 0)
Z_PEERS = sorted(range(1, NZ), key=lambda o: -ring(o, NZ))
MP_PEERS = sorted(
    [(b, c) for b in range(NX) for c in range(NC) if (b, c) != (0, 0)],
    key=lambda o: -ring(o[0], NX),
)


def split3(x):
    hi = x.astype(BF16)
    rest = x - hi.astype(F32)
    mid = rest.astype(BF16)
    low = (rest - mid.astype(F32)).astype(BF16)
    return hi, mid, low


def stack3(x):
    return jnp.concatenate(split3(x), axis=0)


def lay(x, order):
    parts = split3(x)
    return jnp.concatenate([parts[i] for i in order] + [jnp.zeros_like(parts[0])] * 2, axis=0)


LEFT_PARTS = (0, 0, 1, 1, 0, 2)
RIGHT_PARTS = (0, 1, 0, 1, 2, 0)
ERR0_CUTS = 2


def sum3(x):
    n = x.shape[0] // 3
    return x[:n] + (x[n : 2 * n] + x[2 * n :])


def dot(a, b, ca, cb):
    return lax.dot_general(a, b, (((ca,), (cb,)), ((), ())), preferred_element_type=F32)


def dot_high(a, b, ca, cb):
    return lax.dot_general(
        a, b, (((ca,), (cb,)), ((), ())), precision=HIGHEST, preferred_element_type=F32
    )


def chunk(index):
    row = pl.multiple_of((index // 8) * CB, CB)
    lane = pl.multiple_of(lax.rem(index, 8) * CL, CL)
    return pl.ds(row, CB), pl.ds(lane, CL)


def inverse_factors(gram):
    lane = lax.broadcasted_iota(jnp.int32, (R, 128), 1)
    row = lax.broadcasted_iota(jnp.int32, (R, 128), 0)
    first = lax.rem(lane // R, 2) == 0
    unit = jnp.where(lax.rem(lane, R) == row, 1.0, 0.0).astype(F32)
    w = jnp.where(lane < 2 * R, gram, unit)
    for k in range(R - 1):
        pivot_row = w[k : k + 1, :]
        f0 = w[:, k : k + 1] / pivot_row[:, k : k + 1]
        f1 = w[:, R + k : R + k + 1] / pivot_row[:, R + k : R + k + 1]
        factor = jnp.where(first, f0, f1)
        w = w - jnp.where(row > k, factor * pivot_row, 0.0)
    on0 = jnp.sum(jnp.where(lane == row, w, 0.0), axis=1, keepdims=True)
    on1 = jnp.sum(jnp.where(lane == row + R, w, 0.0), axis=1, keepdims=True)
    w = w * jnp.where(first, 1.0 / jnp.sqrt(on0), 1.0 / jnp.sqrt(on1))
    return w[:, 2 * R : 3 * R], w[:, 3 * R : 4 * R]


def exchange(
    a_hbm, g_hbm, f_hbm, qt_hbm, err0, mat1, left1, q_full, inv,
    a, g, f, qt, at, mat0, left0, mhi, mlo, p_part, p_recv, p_full,
    gram_own, gram_recv, q_part, q_recv, z_recv,
    load_sem, send_sem, recv_sem,
):
    dp, mp = lax.axis_index("dp"), lax.axis_index("mp")
    y, z, x, c = dp // NZ, lax.rem(dp, NZ), mp // NC, lax.rem(mp, NC)
    block_id = y * 8 + mp

    def dp_target(o):
        return (lax.rem(y + o[0], NY) * NZ + lax.rem(z + o[1], NZ), mp)

    def block_target(o):
        return (
            lax.rem(y + o[0], NY) * NZ + z,
            lax.rem(x + o[1], NX) * NC + lax.rem(c + o[2], NC),
        )

    def z_target(o):
        return (y * NZ + lax.rem(z + o, NZ), mp)

    half = [pl.ds(m * KVW, KVW) for m in range(2)]
    loads = {}

    def load(name, src, dst):
        loads[name] = pltpu.make_async_copy(src, dst, load_sem.at[len(loads)])
        loads[name].start()

    load("q", qt_hbm, qt)
    for m in range(2):
        load(f"g{m}", g_hbm.at[:, half[m]], g.at[pl.ds(0, TOK), half[m]])
        load(f"f{m}", f_hbm.at[:, half[m]], f.at[:, half[m]])
        if m == 0:
            load("a", a_hbm, a.at[pl.ds(0, TOK), :])
    barrier = pltpu.get_barrier_semaphore()
    greeted = [dp_target(o) for o in DP_PEERS]
    greeted += [block_target(o) for o in BLOCK_PEERS if o[1:] != (0, 0)]
    for target in greeted:
        pl.semaphore_signal(barrier, inc=1, device_id=target, device_id_type=MESH)

    g[TOK:, :] = jnp.zeros((TOK_PAD - TOK, WIDTH), BF16)
    a[TOK:, :] = jnp.zeros((TOK_PAD - TOK, ROWS), BF16)

    def arrival(dz, m):
        opposite = lax.rem(lax.rem(z + dz, NZ) // 2 + 2, 4) == z // 2
        return jnp.where(opposite, 11 + m, 2 + m)

    def send(src, dst, target, which, arrives=None):
        pltpu.make_async_remote_copy(
            src_ref=src,
            dst_ref=dst,
            send_sem=send_sem.at[which],
            recv_sem=recv_sem.at[which if arrives is None else arrives],
            device_id=target,
            device_id_type=MESH,
        ).start()

    def wait_on(sem, view):
        pltpu.make_async_copy(view, view, sem).wait()

    def left_factors(m):
        cols = slice(m * KVW, (m + 1) * KVW)
        q3 = stack3(qt[pl.ds(m * R, R), :])
        loads[f"g{m}"].wait()
        inner3 = stack3(sum3(dot(q3, g[:, cols], 1, 1)))
        loads[f"f{m}"].wait()
        part = sum3(dot(q3, f[:, cols], 1, 1))
        if m == 0:
            loads["a"].wait()
        p_part[m] = part + sum3(dot(inner3, a[...], 1, 0))

    loads["q"].wait()
    for m in range(2):
        pl.when(dp >= 0)(functools.partial(left_factors, m))
        if m == 0:
            pl.semaphore_wait(barrier, len(greeted))
        for i, o in enumerate(DP_PEERS):
            target = dp_target(o)
            row, lane = chunk(target[0])
            send(p_part.at[m, row, lane], p_recv.at[m, i], target, m)

    at[...] = a[...].T

    def columns(n):
        m, lanes = n // 2, slice(n * 512, (n + 1) * 512)
        block = dot(at[...], g[:, lanes], 1, 0) + f[:, lanes].astype(F32)
        (mat0, mat1)[m][:, (n % 2) * 512 : (n % 2 + 1) * 512] = block
        hi = block.astype(BF16)
        mhi[:, lanes] = hi
        mlo[:, lanes] = (block - hi.astype(F32)).astype(BF16)

    row, lane = chunk(dp)
    for m in range(2):
        columns(m)
        wait_on(recv_sem.at[m], p_recv.at[m])
        own = p_part[m, row, lane]
        for i in range(N_PEERS):
            own = own + p_recv[m, i]
        p_full[m, row, lane] = own * (1.0 / 32)
        mine = p_full.at[m, row, lane]
        for o in DP_PEERS:
            send(mine, mine, dp_target(o), 2 + m, arrival(o[1], m))
    columns(2)
    columns(3)

    for m in range(2):
        terms = []
        for step in (1, 3, 0, 2):
            if step == 1:
                wait_on(recv_sem.at[2 + m], p_recv.at[m, pl.ds(0, N_PEERS - 8)])
            if step == 2:
                wait_on(recv_sem.at[11 + m], p_recv.at[m, pl.ds(0, 8)])
            pair = lax.rem(z // 2 + step, 4)
            wide = pl.ds(pl.multiple_of(pair * 256, 256), 256)
            cols = slice(m * KVW, (m + 1) * KVW)
            p3 = stack3(p_full[m, :, wide])
            terms.append(dot(p3, mhi[wide, cols], 1, 0) + dot(p3, mlo[wide, cols], 1, 0))
        q_part[m] = sum3(terms[0] + terms[1] + terms[2] + terms[3])
        for i, o in enumerate(BLOCK_PEERS):
            target = block_target(o)
            r, l = chunk((target[0] // NZ) * 8 + target[1])
            send(q_part.at[m, r, l], q_recv.at[m, i], target, 4 + m)

    lane64 = lax.broadcasted_iota(jnp.int32, (R, 2 * R), 1)
    p_all = jnp.concatenate([p_full[0], p_full[1]], axis=0)
    both = dot_high(p_all, p_all, 1, 1)
    terms = jnp.where(lane64 < R, both[:R], both[R:])
    gram_own[...] = jnp.concatenate([terms, jnp.zeros((R, 128 - 2 * R), F32)], axis=1)
    for o in MP_PEERS:
        send(gram_own, gram_recv.at[mp], block_target((0,) + o), 10)
    gram_recv[mp] = gram_own[...]

    row, lane = chunk(block_id)
    for m in range(2):
        wait_on(recv_sem.at[4 + m], q_recv.at[m])
        own = q_part[m, row, lane]
        for i in range(N_PEERS):
            own = own + q_recv[m, i]
        z_recv[m, z] = own
        for o in Z_PEERS:
            send(z_recv.at[m, z], z_recv.at[m, z], z_target(o), 6 + m)

    wait_on(recv_sem.at[10], gram_recv.at[pl.ds(0, 7)])
    gram = gram_recv[0]
    for i in range(1, 8):
        gram = gram + gram_recv[i]
    inverses = inverse_factors(gram)

    for m in range(2):
        wait_on(recv_sem.at[6 + m], z_recv.at[m, pl.ds(0, 7)])
        own = z_recv[m, 0]
        for i in range(1, NZ):
            own = own + z_recv[m, i]
        q_full[m, row, lane] = own * (1.0 / 32)
        mine = q_full.at[m, row, lane]
        for o in BLOCK_PEERS:
            send(mine, mine, block_target(o), 8 + m)

    for m in range(2):
        wait_on(send_sem.at[m], p_recv.at[m])
        wait_on(send_sem.at[2 + m], p_recv.at[m])
        wait_on(send_sem.at[4 + m], q_recv.at[m])
        wait_on(send_sem.at[6 + m], z_recv.at[m, pl.ds(0, 7)])
    wait_on(send_sem.at[10], gram_recv.at[pl.ds(0, 7)])

    inv[0] = inverses[0]
    inv[1] = inverses[1]
    for m in range(2):
        normed = dot_high(inverses[m], p_full[m], 1, 0)
        left = dot_high(inverses[m], normed, 0, 0)
        (left0, left1)[m][...] = lay(left, LEFT_PARTS).T

    wait_on(recv_sem.at[8], q_recv.at[0])
    raw = q_full[0]
    laid = lay(raw, RIGHT_PARTS)
    for i in range(4):
        rows = pl.ds(i * 256, 256)
        err0[rows, :] = (mat0[rows, :] - dot(left0[rows, :], laid, 1, 0)).astype(BF16)
    wait_on(recv_sem.at[9], q_recv.at[1])

    for m in range(2):
        wait_on(send_sem.at[8 + m], q_recv.at[m])


def finish(err0, mat1, left1, q_full, inv, err_hbm, qn_hbm, err1, qn, out_sem):
    outs = []

    def store(src, dst):
        outs.append(pltpu.make_async_copy(src, dst, out_sem.at[len(outs)]))
        outs[-1].start()

    for i in range(ERR0_CUTS):
        rows = pl.ds(i * (ROWS // ERR0_CUTS), ROWS // ERR0_CUTS)
        store(err0.at[rows, :], err_hbm.at[rows, pl.ds(0, KVW)])
    laid = lay(q_full[1], RIGHT_PARTS)
    for i in range(8):
        rows = pl.ds(i * 128, 128)
        err1[rows, :] = (mat1[rows, :] - dot(left1[rows, :], laid, 1, 0)).astype(BF16)
        store(err1.at[rows, :], err_hbm.at[rows, pl.ds(KVW, KVW)])
    for m in range(2):
        qn[pl.ds(m * R, R), :] = dot_high(inv[m], q_full[m], 1, 0)
    store(qn, qn_hbm)
    for copy in outs:
        copy.wait()


def per_device(activations, out_grads, feedback, q_prev):
    qt = jnp.transpose(q_prev, (1, 2, 0)).reshape(2 * R, KVW)
    any_space = pl.BlockSpec(memory_space=pl.ANY)
    vmem = pl.BlockSpec(memory_space=pltpu.VMEM)
    held = pl.pallas_call(
        exchange,
        out_shape=(
            pltpu.VMEM((ROWS, KVW), BF16),
            pltpu.VMEM((ROWS, KVW), F32),
            pltpu.VMEM((ROWS, 256), BF16),
            pltpu.VMEM((2, R, KVW), F32),
            pltpu.VMEM((2, R, R), F32),
        ),
        in_specs=[any_space] * 4,
        out_specs=(vmem,) * 5,
        scratch_shapes=[
            pltpu.VMEM((TOK_PAD, ROWS), BF16),
            pltpu.VMEM((TOK_PAD, WIDTH), BF16),
            pltpu.VMEM((ROWS, WIDTH), BF16),
            pltpu.VMEM((2 * R, KVW), F32),
            pltpu.VMEM((ROWS, TOK_PAD), BF16),
            pltpu.VMEM((ROWS, KVW), F32),
            pltpu.VMEM((ROWS, 256), BF16),
            pltpu.VMEM((ROWS, WIDTH), BF16),
            pltpu.VMEM((ROWS, WIDTH), BF16),
            pltpu.VMEM((2, R, ROWS), F32),
            pltpu.VMEM((2, N_PEERS, CB, CL), F32),
            pltpu.VMEM((2, R, ROWS), F32),
            pltpu.VMEM((R, 128), F32),
            pltpu.VMEM((8, R, 128), F32),
            pltpu.VMEM((2, R, KVW), F32),
            pltpu.VMEM((2, N_PEERS, CB, CL), F32),
            pltpu.VMEM((2, NZ, CB, CL), F32),
            pltpu.SemaphoreType.DMA((10,)),
            pltpu.SemaphoreType.DMA((11,)),
            pltpu.SemaphoreType.DMA((13,)),
        ],
        compiler_params=pltpu.CompilerParams(
            collective_id=0, has_side_effects=True, vmem_limit_bytes=40 * 2**20
        ),
    )(*[pltpu.with_memory_space_constraint(v, pltpu.HBM) for v in (activations, out_grads, feedback[0], qt)])
    err, qn = pl.pallas_call(
        finish,
        out_shape=(
            jax.ShapeDtypeStruct((ROWS, WIDTH), BF16),
            jax.ShapeDtypeStruct((2 * R, KVW), F32),
        ),
        in_specs=[vmem] * 5,
        out_specs=(any_space,) * 2,
        scratch_shapes=[
            pltpu.VMEM((ROWS, KVW), BF16),
            pltpu.VMEM((2 * R, KVW), F32),
            pltpu.SemaphoreType.DMA((ERR0_CUTS + 9,)),
        ],
        compiler_params=pltpu.CompilerParams(vmem_limit_bytes=24 * 2**20),
    )(*held)
    q_new = jnp.transpose(qn.reshape(2, R, KVW), (2, 0, 1))
    return err[None], q_new


def solution(mesh):
    return jax.shard_map(
        per_device,
        mesh=mesh,
        in_specs=(P("dp", "mp"), P("dp", None), P("dp", "mp", None), P()),
        out_specs=(P("dp", "mp", None), P()),
        check_vma=False,
    )
```
